32 devices in a mesh: parts: 2 (over y), gy: 8 (over z, x), gz: 2 (over core).
Axes of the slice: x: 2, y: 2, z: 4, core: 2. Of those that a mesh axis runs over, the one named last changes fastest.
Arguments:
- volume: bfloat16 [32, 64, 4096], P(('parts', 'gz'), 'gy'), parts along dimension 0, may hold values from 0 to 1
- column_weight: float32 [8, 64], P('parts', 'gy'), parts along dimension 0, may hold values from 0.02 to 0.2
- tile_xblock: int32 [8, 8, 32, 6], P('parts', 'gy'), parts along dimension 0, may hold values from 0 to 31, as said below
- tile_bank: int32 [8, 8, 32, 6], P('parts', 'gy'), parts along dimension 0, may hold values from 0 to 15
- tile_count: int32 [8, 8, 32], P('parts', 'gy'), parts along dimension 0, may hold values from 1 to 6, as said below
- footprint: bfloat16 [16, 128, 128], replicated, may hold values from -0.375 to 0.375
- cone_extent: int32 [8, 4096], P('parts', 'gy'), parts along dimension 0, may hold values from 1 to 4
- measured: float32 [8, 16, 4096], P('parts', 'gz', 'gy'), parts along dimension 0, may hold values from -8 to 8
- ray_length: float32 [8, 16, 4096], P('parts', 'gz', 'gy'), parts along dimension 0, may hold values from 0.5 to 2
Outputs:
- new_volume: bfloat16 [32, 64, 4096], P(('parts', 'gz'), 'gy'), parts along dimension 0
- back_rows: float32 [8, 16, 4096], P('parts', 'gz', 'gy'), parts along dimension 0
The draws below stay inside these ranges and needn't reach their ends.
There are 2 independent parts, one for each index of `parts`. The reference program is written for one: setup_inputs(seed, part) draws one part's arguments, and reference() takes and returns one part's arrays. A program takes and returns all parts, laid end to end along the dimension named above; an argument that names none is the same for every part. Nothing has to cross between parts.
Inputs may be any that keep to these rules, and one draw needn't show every extreme that they name: Slots s >= tile_count of a list hold valid entries that are not used; a list's used slots are most numerous at central y groups and central detector tiles. `tile_xblock`: an x tile index.
All inputs are finite; a program needn't handle non-finite values.
Results may differ from the reference program's by a relative error of at most 0.0052.
Values may be sent and summed in bfloat16 or wider, within the bound.
A program may use at most 64 MiB of HBM per device.

```python
import math
import jax
import jax.numpy as jnp
from jax import lax

NX = 4096
YC = 8
ANGLES = 4
SLOTS = 6
BANK = 16
TILE = 128
REACH = 4
NY = 64
NZ = 16
NXT = 32
GROUPS = 8


def draw_tile_xblock(key, part):
    key = jax.random.fold_in(key, 11)
    tiles = jnp.arange(NXT, dtype=jnp.int32)[None, None, :, None]
    slots = jnp.arange(SLOTS, dtype=jnp.int32)[None, None, None, :]
    jitter = jax.random.randint(key, (ANGLES, GROUPS, NXT, SLOTS), -1, 2)
    return ((tiles + slots - SLOTS // 2 + jitter) % NXT).astype(jnp.int32)


def draw_tile_count(key, part):
    key = jax.random.fold_in(key, 23)
    first, second = jax.random.split(key)
    shape = (ANGLES, GROUPS, NXT)
    light = jax.random.randint(first, shape, 1, 3)
    heavy = jax.random.randint(second, shape, SLOTS - 1, SLOTS + 1)
    groups = jnp.arange(GROUPS, dtype=jnp.int32)[None, :, None]
    tiles = jnp.arange(NXT, dtype=jnp.int32)[None, None, :]
    central = (groups >= GROUPS // 4) & (groups < 3 * GROUPS // 4) & (tiles >= NXT // 4) & (tiles < 3 * NXT // 4)
    counts = jnp.where(central, heavy, light).astype(jnp.int32)
    return counts.at[0, GROUPS // 2, NXT // 2].set(SLOTS)


def place_ends(entries, key, smallest, high):
    longest = entries.shape.index(max(entries.shape))
    spots = []
    for shift in (0, 1):
        where = [jax.random.randint(jax.random.fold_in(key, axis), (), 0, length) for axis, length in enumerate(entries.shape)]
        where[longest] = (where[longest] + shift) % entries.shape[longest]
        spots.append(tuple(where))
    return entries.at[spots[0]].set(smallest).at[spots[1]].set(high)


def block_levels(key, shape, shards, least, high):
    gain = 1.0
    for axis_at, parts in shards:
        steps = jax.random.uniform(jax.random.fold_in(jax.random.fold_in(key, 6), axis_at), (parts,), jnp.float32, least / len(shards), high / len(shards))
        gain = gain * jnp.repeat(jnp.exp(steps), shape[axis_at] // parts).reshape((-1,) + (1,) * (len(shape) - 1 - axis_at))
    return gain


def noise(own_key, shape, scale, most, shards=(), held_as=jnp.bfloat16):
    gain = block_levels(own_key, shape, shards, -0.22, 0.18) if shards else 1.0
    array = jax.random.normal(own_key, shape, jnp.float32) * scale * gain
    return jnp.minimum(jnp.maximum(array, -most), most).astype(held_as)


def setup_inputs(seed: int = 0, part: int = 0) -> dict:
    key_of = jax.random.split(jax.random.key(seed), 10)
    own_keys = jax.random.split(jax.random.fold_in(key_of[9], part), 10)
    return {
        "volume": jnp.clip(1.0 * jax.random.uniform(own_keys[0], (NZ, NY, NX), jnp.float32) ** block_levels(own_keys[0], (NZ, NY, NX), ((0, 2), (1, 8)), -0.2, 0.2), 0.0, 1.0).astype(jnp.bfloat16),
        "column_weight": jnp.clip(jnp.exp(math.log(0.2) - 2.3025851 * jax.random.uniform(own_keys[1], (ANGLES, NY), jnp.float32) ** block_levels(own_keys[1], (ANGLES, NY), ((1, 8),), -0.2, 0.2)), 0.02, 0.2),
        "tile_xblock": draw_tile_xblock(jax.random.fold_in(jax.random.fold_in(key_of[9], part), 71), part),
        "tile_bank": place_ends(jax.random.randint(own_keys[3], (ANGLES, GROUPS, NXT, SLOTS), 0, BANK), jax.random.fold_in(own_keys[3], 1), 0, BANK - 1).astype(jnp.int32),
        "tile_count": draw_tile_count(jax.random.fold_in(jax.random.fold_in(key_of[9], part), 71), part),
        "footprint": noise(key_of[5], (BANK, TILE, TILE), (TILE * 2) ** -0.5, 0.375),
        "cone_extent": place_ends(jax.random.randint(own_keys[6], (ANGLES, NX), 1, REACH + 1), jax.random.fold_in(own_keys[6], 1), 1, REACH).astype(jnp.int32),
        "measured": noise(own_keys[7], (ANGLES, NZ, NX), 2.0, 8.0, ((1, 2), (2, 8)), jnp.float32),
        "ray_length": jnp.clip(jnp.exp(math.log(2.0) - 1.3862944 * jax.random.uniform(own_keys[8], (ANGLES, NZ, NX), jnp.float32) ** block_levels(own_keys[8], (ANGLES, NZ, NX), ((1, 2), (2, 8)), -0.2, 0.2)), 0.5, 2.0),
    }


CONE_WEIGHTS = (0.45, 0.3, 0.2, 0.12)


def cone(signal, extent):
    spread = len(CONE_WEIGHTS)
    depth = signal.shape[1]
    padded = jnp.pad(signal, ((0, 0), (spread, spread), (0, 0)))
    summed = signal
    for offset in range(1, spread + 1):
        gating = (extent >= offset).astype(jnp.float32)[:, None, :]
        beside_all = padded[:, spread - offset:spread - offset + depth] + padded[:, spread + offset:spread + offset + depth]
        summed = summed + CONE_WEIGHTS[offset - 1] * gating * beside_all
    return summed


def weighted(columns, weights):
    return jnp.sum(columns.astype(jnp.float32) * weights[None, :, None], axis=1).astype(jnp.bfloat16)


def slot_usable(filled):
    return jnp.arange(SLOTS)[None, :] < filled[:, None]


def forward_ref(rows_in, xblock, bank_ids, filled, footprint):
    depth = rows_in.shape[0]
    blocks = rows_in.reshape(depth, -1, TILE).transpose(1, 0, 2)
    usable = slot_usable(filled).astype(jnp.bfloat16)
    left_tiles = blocks[xblock] * usable[:, :, None, None]
    right_tiles = footprint[bank_ids]
    products = jnp.einsum('tszj,tsji->tzi', left_tiles.astype(jnp.float32), right_tiles.astype(jnp.float32))
    return products.transpose(1, 0, 2).reshape(depth, -1)


def back_ref(sent_rows, xblock, bank_ids, filled, footprint):
    depth = sent_rows.shape[0]
    blocks = sent_rows.reshape(depth, -1, TILE).transpose(1, 0, 2)
    right_tiles = footprint[bank_ids]
    spread_out = jnp.einsum('tzi,tsji->tszj', blocks.astype(jnp.float32), right_tiles.astype(jnp.float32))
    spread_out = spread_out * slot_usable(filled).astype(jnp.float32)[:, :, None, None]
    summed = jnp.zeros((blocks.shape[0], depth, TILE), jnp.float32)
    summed = summed.at[xblock.reshape(-1)].add(spread_out.reshape(-1, depth, TILE))
    return summed.transpose(1, 0, 2).reshape(depth, -1)


def reference(volume, column_weight, tile_xblock, tile_bank, tile_count, footprint, cone_extent, measured, ray_length):
    def accumulate(partial_value, group_no):
        columns = lax.dynamic_slice_in_dim(volume, group_no * YC, YC, 1)
        weights = lax.dynamic_slice_in_dim(column_weight, group_no * YC, YC, 1)
        pieces = []
        for angle_no in range(ANGLES):
            rows_in = weighted(columns, weights[angle_no])
            pieces.append(forward_ref(rows_in, tile_xblock[angle_no, group_no], tile_bank[angle_no, group_no], tile_count[angle_no, group_no], footprint))
        return partial_value + jnp.stack(pieces), None

    start = jnp.zeros((ANGLES, NZ, NX), jnp.float32)
    projected, unused = lax.scan(accumulate, start, jnp.arange(GROUPS, dtype=jnp.int32))
    predicted = cone(projected, cone_extent)
    mismatch = (measured - predicted) / ray_length
    back_rows = cone(mismatch, cone_extent)
    sent = back_rows.astype(jnp.bfloat16)

    def update(group_no):
        columns = lax.dynamic_slice_in_dim(volume, group_no * YC, YC, 1)
        weights = lax.dynamic_slice_in_dim(column_weight, group_no * YC, YC, 1)
        change = jnp.zeros((NZ, YC, NX), jnp.float32)
        for angle_no in range(ANGLES):
            spread_back = back_ref(sent[angle_no], tile_xblock[angle_no, group_no], tile_bank[angle_no, group_no], tile_count[angle_no, group_no], footprint)
            change = change + weights[angle_no][None, :, None] * spread_back[:, None, :]
        return jnp.maximum(columns.astype(jnp.float32) + change, 0.0).astype(jnp.bfloat16)

    fresh = lax.map(update, jnp.arange(GROUPS, dtype=jnp.int32))
    new_volume = fresh.transpose(1, 0, 2, 3).reshape(NZ, NY, NX)
    return new_volume, back_rows
```

```python
import functools

import jax
import jax.numpy as jnp
from jax import lax
from jax.experimental import pallas as pl
from jax.experimental.pallas import tpu as pltpu
from jax.sharding import PartitionSpec as P

TILE = 128
ROWS = 8
CONE_WEIGHTS = (0.45, 0.3, 0.2, 0.12)
VMEM_LIMIT = 48 * 2**20
MESH = pl.DeviceIdType.MESH


def extended(cells, axis, dim, width):
    count = lax.axis_size(axis)
    ends = count - 1
    head = lax.slice_in_dim(cells, 0, width, axis=dim)
    tail = lax.slice_in_dim(cells, cells.shape[dim] - width, cells.shape[dim], axis=dim)
    return jnp.concatenate(
        [
            lax.ppermute(tail, axis, [(i, (i + 1) % count) for i in range(ends)]),
            cells,
            lax.ppermute(head, axis, [((i + 1) % count, i) for i in range(ends)]),
        ],
        axis=dim,
    )


def cone_across(signal, extent):
    spread = len(CONE_WEIGHTS)
    depth = signal.shape[1]
    padded = extended(signal, "gz", 1, spread)
    summed = signal
    for offset in range(1, spread + 1):
        gating = (extent >= offset).astype(jnp.float32)[:, None, :]
        beside = (
            padded[:, spread - offset : spread - offset + depth]
            + padded[:, spread + offset : spread + offset + depth]
        )
        summed = summed + CONE_WEIGHTS[offset - 1] * gating * beside
    return summed


def weight_matrix(w_ref, shape, angle_z, z_col):
    angles, cols = w_ref.shape
    a, z = angle_z
    zz, c = z_col
    key = a * cols + c
    out = jnp.zeros(shape, jnp.float32)
    for an in range(angles):
        for cn in range(cols):
            out = jnp.where(key == an * cols + cn, w_ref[an, cn], out)
    return jnp.where(z == zz, out, 0.0)


def split_part(value, part):
    high = value.astype(jnp.bfloat16).astype(jnp.float32)
    rest = value - high
    mid = rest.astype(jnp.bfloat16).astype(jnp.float32)
    return jnp.where(part == 0, high, jnp.where(part == 1, mid, rest - mid)).astype(jnp.bfloat16)


def column_sums(w_ref, vol_ref, lhs_ref):
    angles, cols = w_ref.shape
    depth, _, total = vol_ref.shape
    m = angles * depth
    shape = (3 * m, depth * cols)
    row = lax.broadcasted_iota(jnp.int32, shape, 0)
    col = lax.broadcasted_iota(jnp.int32, shape, 1)
    zb = depth.bit_length() - 1
    cb = cols.bit_length() - 1
    inner = row & (m - 1)
    w = weight_matrix(
        w_ref, shape, (inner >> zb, inner & (depth - 1)), (col >> cb, col & (cols - 1))
    )
    w3 = split_part(w, row >> (m.bit_length() - 1))
    step = 4 * TILE

    def body(i, carry):
        at = pl.ds(pl.multiple_of(i * step, step), step)
        v = jnp.concatenate([vol_ref[z, :, at].astype(jnp.float32) for z in range(depth)], axis=0)
        r = jnp.dot(w3, v.astype(jnp.bfloat16), preferred_element_type=jnp.float32)
        r = (r[:m] + (r[m : 2 * m] + r[2 * m :])).astype(jnp.bfloat16)
        for k in range(4):
            lhs_ref[pl.ds(pl.multiple_of((i * 4 + k) * m, m), m), :] = r[:, k * TILE : (k + 1) * TILE]
        return carry

    lax.fori_loop(0, total // step, body, 0)


def all_products(lhs_ref, fp_ref, prod_ref, transposed):
    banks = fp_ref.shape[0]
    total = lhs_ref.shape[0]
    blocks = total // ROWS
    chunk = 256
    prod_ref[pl.ds(banks * blocks, blocks)] = jnp.zeros((blocks, ROWS, TILE), jnp.float32)

    def body(i, carry):
        b = 2 * i
        if transposed:
            f = jnp.concatenate([fp_ref[b], fp_ref[b + 1]], axis=0)
            dims = (((1,), (1,)), ((), ()))
        else:
            f = jnp.concatenate([fp_ref[b], fp_ref[b + 1]], axis=1)
            dims = (((1,), (0,)), ((), ()))
        for k in range(total // chunk):
            p = lax.dot_general(
                lhs_ref[k * chunk : (k + 1) * chunk, :], f, dims, preferred_element_type=jnp.float32
            )
            n = chunk // ROWS
            for h in range(2):
                prod_ref[pl.ds((b + h) * blocks + k * n, n)] = p[
                    :, h * TILE : (h + 1) * TILE
                ].reshape(n, ROWS, TILE)
        return carry

    lax.fori_loop(0, banks // 2, body, 0)


def ray_sum(idx_ref, prod_ref, t, angles, tiles, slots):
    parts = []
    for a in range(angles):
        at = (a * tiles + t) * slots
        terms = [prod_ref[idx_ref[at + s]] for s in range(slots)]
        while len(terms) > 1:
            terms = [sum(terms[i : i + 2][1:], terms[i]) for i in range(0, len(terms), 2)]
        parts.append(terms[0])
    return jnp.concatenate(parts, axis=0)


def packed_slots(xblock, bank, count, banks):
    angles, _, tiles, slots = xblock.shape
    used = jnp.arange(slots)[None, None, :] < count[:, 0, :, None]
    b = jnp.where(used, bank[:, 0], banks)
    angle = jnp.arange(angles, dtype=jnp.int32)[:, None, None]
    return (b * (tiles * angles) + xblock[:, 0] * angles + angle).reshape(-1)


def back_kernel(idx_ref, w_ref, sent_ref, fp_ref, vol_ref, out_ref, lhs_ref, prod_ref, *acc_refs):
    angles, cols = w_ref.shape
    depth, _, total = vol_ref.shape
    tiles = total // TILE
    slots = idx_ref.shape[0] // (angles * tiles)
    m = angles * depth
    per = sent_ref.shape[2] // TILE
    for t in range(tiles):
        lhs_ref[t * m : (t + 1) * m, :] = sent_ref[t // per, :, (t % per) * TILE : (t % per + 1) * TILE]
    all_products(lhs_ref, fp_ref, prod_ref, True)
    for acc in acc_refs:
        acc[...] = jnp.zeros_like(acc)
    mask = tiles * angles - 1

    def body(t, carry):
        for s in range(slots):
            for a in range(angles):
                packed = idx_ref[(a * tiles + t) * slots + s]
                low = packed & mask
                x = low >> (angles.bit_length() - 1)
                acc_refs[a][x] += prod_ref[packed - low + (t * angles + a)]
        return carry

    lax.fori_loop(0, tiles, body, 0)

    shape = (depth * cols, 3 * m)
    row = lax.broadcasted_iota(jnp.int32, shape, 0)
    col = lax.broadcasted_iota(jnp.int32, shape, 1)
    zb = depth.bit_length() - 1
    cb = cols.bit_length() - 1
    inner = col & (m - 1)
    for extra in (1, 2):
        inner = jnp.where(col >= extra * m, (col - extra * m) & (m - 1), inner)
    w = weight_matrix(
        w_ref, shape, (inner >> zb, inner & (depth - 1)), (row >> cb, row & (cols - 1))
    )
    w3 = split_part(w, jnp.where(col >= 2 * m, 1, 0))
    step = 4

    def finish(i, carry):
        s = jnp.concatenate(
            [
                jnp.concatenate([acc_refs[a][i * step + k] for k in range(step)], axis=1)
                for a in range(angles)
            ],
            axis=0,
        )
        high = s.astype(jnp.bfloat16)
        low = (s - high.astype(jnp.float32)).astype(jnp.bfloat16)
        change = jnp.dot(
            w3, jnp.concatenate([high, low, high], axis=0), preferred_element_type=jnp.float32
        )
        at = pl.ds(pl.multiple_of(i * step * TILE, step * TILE), step * TILE)
        for z in range(depth):
            fresh = vol_ref[z, :, at].astype(jnp.float32) + change[z * cols : (z + 1) * cols]
            out_ref[z, :, at] = jnp.maximum(fresh, 0.0).astype(jnp.bfloat16)
        return carry

    lax.fori_loop(0, tiles // step, finish, 0)


SMEM = pl.BlockSpec(memory_space=pltpu.SMEM)
VMEM = pl.BlockSpec(memory_space=pltpu.VMEM)


def back(packed, column_weight, sent, footprint, volume):
    angles = column_weight.shape[0]
    depth, _, total = volume.shape
    tiles = total // TILE
    banks = footprint.shape[0]
    rows = tiles * angles * depth
    return pl.pallas_call(
        back_kernel,
        out_shape=jax.ShapeDtypeStruct(volume.shape, jnp.bfloat16),
        in_specs=[SMEM, SMEM, VMEM, VMEM, VMEM],
        out_specs=VMEM,
        scratch_shapes=[
            pltpu.VMEM((rows, TILE), jnp.bfloat16),
            pltpu.VMEM(((banks + 1) * tiles * angles, ROWS, TILE), jnp.float32),
        ]
        + [pltpu.VMEM((tiles, ROWS, TILE), jnp.float32) for _ in range(angles)],
        compiler_params=pltpu.CompilerParams(vmem_limit_bytes=VMEM_LIMIT),
        name="back_spread",
    )(packed, column_weight, sent, footprint, volume)


def forward_kernel(idx_ref, w_ref, fp_ref, vol_ref, out_ref, lhs_ref, prod_ref):
    angles = w_ref.shape[0]
    tiles = vol_ref.shape[2] // TILE
    slots = idx_ref.shape[0] // (angles * tiles)
    column_sums(w_ref, vol_ref, lhs_ref)
    all_products(lhs_ref, fp_ref, prod_ref, False)

    def body(t, carry):
        out_ref[:, pl.ds(pl.multiple_of(t * TILE, TILE), TILE)] = ray_sum(
            idx_ref, prod_ref, t, angles, tiles, slots
        )
        return carry

    lax.fori_loop(0, tiles, body, 0)


def forward(packed, column_weight, footprint, volume):
    angles = column_weight.shape[0]
    depth, _, total = volume.shape
    tiles = total // TILE
    banks = footprint.shape[0]
    rows = tiles * angles * depth
    return pl.pallas_call(
        forward_kernel,
        out_shape=jax.ShapeDtypeStruct((angles * depth, total), jnp.float32),
        in_specs=[SMEM, SMEM, VMEM, VMEM],
        out_specs=VMEM,
        scratch_shapes=[
            pltpu.VMEM((rows, TILE), jnp.bfloat16),
            pltpu.VMEM(((banks + 1) * tiles * angles, ROWS, TILE), jnp.float32),
        ],
        compiler_params=pltpu.CompilerParams(vmem_limit_bytes=VMEM_LIMIT),
        name="ray_sums",
    )(packed, column_weight, footprint, volume)


def shards(
    volume,
    column_weight,
    tile_xblock,
    tile_bank,
    tile_count,
    footprint,
    cone_extent,
    measured,
    ray_length,
):
    angles = column_weight.shape[0]
    depth, _, total = volume.shape
    packed = packed_slots(tile_xblock, tile_bank, tile_count, footprint.shape[0])
    partial = forward(packed, column_weight, footprint, volume).reshape(angles, depth, total)
    owned = lax.psum_scatter(partial, "gy", scatter_dimension=2, tiled=True)
    predicted = cone_across(owned, cone_extent)
    back_rows = cone_across((measured - predicted) / ray_length, cone_extent)
    sent = lax.all_gather(back_rows.astype(jnp.bfloat16), "gy", axis=2, tiled=True)
    new_volume = back(
        packed, column_weight, sent.reshape(1, angles * depth, total), footprint, volume
    )
    return new_volume, back_rows


def solution(mesh):
    in_specs = (
        P(("parts", "gz"), "gy", None),
        P("parts", "gy"),
        P("parts", "gy", None, None),
        P("parts", "gy", None, None),
        P("parts", "gy", None),
        P(),
        P("parts", "gy"),
        P("parts", "gz", "gy"),
        P("parts", "gz", "gy"),
    )
    out_specs = (P(("parts", "gz"), "gy", None), P("parts", "gz", "gy"))
    return jax.shard_map(shards, mesh=mesh, in_specs=in_specs, out_specs=out_specs, check_vma=False)
```

```python
import functools

import jax
import jax.numpy as jnp
from jax import lax
from jax.experimental import pallas as pl
from jax.experimental.pallas import tpu as pltpu
from jax.sharding import PartitionSpec as P

TILE = 128
ROWS = 8
CONE_WEIGHTS = (0.45, 0.3, 0.2, 0.12)
VMEM_LIMIT = 48 * 2**20
MESH = pl.DeviceIdType.MESH


def extended(cells, axis, dim, width):
    count = lax.axis_size(axis)
    ends = count - 1
    head = lax.slice_in_dim(cells, 0, width, axis=dim)
    tail = lax.slice_in_dim(cells, cells.shape[dim] - width, cells.shape[dim], axis=dim)
    return jnp.concatenate(
        [
            lax.ppermute(tail, axis, [(i, (i + 1) % count) for i in range(ends)]),
            cells,
            lax.ppermute(head, axis, [((i + 1) % count, i) for i in range(ends)]),
        ],
        axis=dim,
    )


def cone_across(signal, extent):
    spread = len(CONE_WEIGHTS)
    depth = signal.shape[1]
    padded = extended(signal, "gz", 1, spread)
    summed = signal
    for offset in range(1, spread + 1):
        gating = (extent >= offset).astype(jnp.float32)[:, None, :]
        beside = (
            padded[:, spread - offset : spread - offset + depth]
            + padded[:, spread + offset : spread + offset + depth]
        )
        summed = summed + CONE_WEIGHTS[offset - 1] * gating * beside
    return summed


def weight_matrix(w_ref, shape, angle_z, z_col):
    angles, cols = w_ref.shape
    a, z = angle_z
    zz, c = z_col
    key = a * cols + c
    out = jnp.zeros(shape, jnp.float32)
    for an in range(angles):
        for cn in range(cols):
            out = jnp.where(key == an * cols + cn, w_ref[an, cn], out)
    return jnp.where(z == zz, out, 0.0)


def split_part(value, part):
    high = value.astype(jnp.bfloat16).astype(jnp.float32)
    rest = value - high
    mid = rest.astype(jnp.bfloat16).astype(jnp.float32)
    return jnp.where(part == 0, high, jnp.where(part == 1, mid, rest - mid)).astype(jnp.bfloat16)


def column_sums(w_ref, vol_ref, lhs_ref):
    angles, cols = w_ref.shape
    depth, _, total = vol_ref.shape
    m = angles * depth
    shape = (3 * m, depth * cols)
    row = lax.broadcasted_iota(jnp.int32, shape, 0)
    col = lax.broadcasted_iota(jnp.int32, shape, 1)
    zb = depth.bit_length() - 1
    cb = cols.bit_length() - 1
    inner = row & (m - 1)
    w = weight_matrix(
        w_ref, shape, (inner >> zb, inner & (depth - 1)), (col >> cb, col & (cols - 1))
    )
    w3 = split_part(w, row >> (m.bit_length() - 1))
    step = 4 * TILE

    def body(i, carry):
        at = pl.ds(pl.multiple_of(i * step, step), step)
        v = jnp.concatenate([vol_ref[z, :, at].astype(jnp.float32) for z in range(depth)], axis=0)
        r = jnp.dot(w3, v.astype(jnp.bfloat16), preferred_element_type=jnp.float32)
        r = (r[:m] + (r[m : 2 * m] + r[2 * m :])).astype(jnp.bfloat16)
        for k in range(4):
            lhs_ref[pl.ds(pl.multiple_of((i * 4 + k) * m, m), m), :] = r[:, k * TILE : (k + 1) * TILE]
        return carry

    lax.fori_loop(0, total // step, body, 0)


def all_products(lhs_ref, fp_ref, prod_ref, transposed):
    banks = fp_ref.shape[0]
    total = lhs_ref.shape[0]
    blocks = total // ROWS
    chunk = 256
    prod_ref[pl.ds(banks * blocks, blocks)] = jnp.zeros((blocks, ROWS, TILE), jnp.float32)

    def body(i, carry):
        b = 2 * i
        if transposed:
            f = jnp.concatenate([fp_ref[b], fp_ref[b + 1]], axis=0)
            dims = (((1,), (1,)), ((), ()))
        else:
            f = jnp.concatenate([fp_ref[b], fp_ref[b + 1]], axis=1)
            dims = (((1,), (0,)), ((), ()))
        for k in range(total // chunk):
            p = lax.dot_general(
                lhs_ref[k * chunk : (k + 1) * chunk, :], f, dims, preferred_element_type=jnp.float32
            )
            n = chunk // ROWS
            for h in range(2):
                prod_ref[pl.ds((b + h) * blocks + k * n, n)] = p[
                    :, h * TILE : (h + 1) * TILE
                ].reshape(n, ROWS, TILE)
        return carry

    lax.fori_loop(0, banks // 2, body, 0)


def ray_sum(idx_ref, prod_ref, t, angles, tiles, slots):
    parts = []
    for a in range(angles):
        at = (a * tiles + t) * slots
        terms = [prod_ref[idx_ref[at + s]] for s in range(slots)]
        while len(terms) > 1:
            terms = [sum(terms[i : i + 2][1:], terms[i]) for i in range(0, len(terms), 2)]
        parts.append(terms[0])
    return jnp.concatenate(parts, axis=0)


def packed_slots(xblock, bank, count, banks):
    angles, _, tiles, slots = xblock.shape
    used = jnp.arange(slots)[None, None, :] < count[:, 0, :, None]
    b = jnp.where(used, bank[:, 0], banks)
    angle = jnp.arange(angles, dtype=jnp.int32)[:, None, None]
    return (b * (tiles * angles) + xblock[:, 0] * angles + angle).reshape(-1)


def back_kernel(idx_ref, w_ref, sent_ref, fp_ref, vol_ref, out_ref, lhs_ref, prod_ref, *acc_refs):
    angles, cols = w_ref.shape
    depth, _, total = vol_ref.shape
    tiles = total // TILE
    slots = idx_ref.shape[0] // (angles * tiles)
    m = angles * depth
    per = sent_ref.shape[2] // TILE
    for t in range(tiles):
        lhs_ref[t * m : (t + 1) * m, :] = sent_ref[t // per, :, (t % per) * TILE : (t % per + 1) * TILE]
    all_products(lhs_ref, fp_ref, prod_ref, True)
    for acc in acc_refs:
        acc[...] = jnp.zeros_like(acc)
    mask = tiles * angles - 1

    def body(t, carry):
        for s in range(slots):
            for a in range(angles):
                packed = idx_ref[(a * tiles + t) * slots + s]
                low = packed & mask
                x = low >> (angles.bit_length() - 1)
                acc_refs[a][x] += prod_ref[packed - low + (t * angles + a)]
        return carry

    lax.fori_loop(0, tiles, body, 0)

    shape = (depth * cols, 3 * m)
    row = lax.broadcasted_iota(jnp.int32, shape, 0)
    col = lax.broadcasted_iota(jnp.int32, shape, 1)
    zb = depth.bit_length() - 1
    cb = cols.bit_length() - 1
    inner = col & (m - 1)
    for extra in (1, 2):
        inner = jnp.where(col >= extra * m, (col - extra * m) & (m - 1), inner)
    w = weight_matrix(
        w_ref, shape, (inner >> zb, inner & (depth - 1)), (row >> cb, row & (cols - 1))
    )
    w3 = split_part(w, jnp.where(col >= 2 * m, 1, 0))
    step = 4

    def finish(i, carry):
        s = jnp.concatenate(
            [
                jnp.concatenate([acc_refs[a][i * step + k] for k in range(step)], axis=1)
                for a in range(angles)
            ],
            axis=0,
        )
        high = s.astype(jnp.bfloat16)
        low = (s - high.astype(jnp.float32)).astype(jnp.bfloat16)
        change = jnp.dot(
            w3, jnp.concatenate([high, low, high], axis=0), preferred_element_type=jnp.float32
        )
        at = pl.ds(pl.multiple_of(i * step * TILE, step * TILE), step * TILE)
        for z in range(depth):
            fresh = vol_ref[z, :, at].astype(jnp.float32) + change[z * cols : (z + 1) * cols]
            out_ref[z, :, at] = jnp.maximum(fresh, 0.0).astype(jnp.bfloat16)
        return carry

    lax.fori_loop(0, tiles // step, finish, 0)


SMEM = pl.BlockSpec(memory_space=pltpu.SMEM)
VMEM = pl.BlockSpec(memory_space=pltpu.VMEM)


def back(packed, column_weight, sent, footprint, volume):
    angles = column_weight.shape[0]
    depth, _, total = volume.shape
    tiles = total // TILE
    banks = footprint.shape[0]
    rows = tiles * angles * depth
    return pl.pallas_call(
        back_kernel,
        out_shape=jax.ShapeDtypeStruct(volume.shape, jnp.bfloat16),
        in_specs=[SMEM, SMEM, VMEM, VMEM, VMEM],
        out_specs=VMEM,
        scratch_shapes=[
            pltpu.VMEM((rows, TILE), jnp.bfloat16),
            pltpu.VMEM(((banks + 1) * tiles * angles, ROWS, TILE), jnp.float32),
        ]
        + [pltpu.VMEM((tiles, ROWS, TILE), jnp.float32) for _ in range(angles)],
        compiler_params=pltpu.CompilerParams(vmem_limit_bytes=VMEM_LIMIT),
        name="back_spread",
    )(packed, column_weight, sent, footprint, volume)


def forward_kernel(idx_ref, w_ref, fp_ref, vol_ref, out_ref, lhs_ref, prod_ref):
    angles = w_ref.shape[0]
    tiles = vol_ref.shape[2] // TILE
    slots = idx_ref.shape[0] // (angles * tiles)
    column_sums(w_ref, vol_ref, lhs_ref)
    all_products(lhs_ref, fp_ref, prod_ref, False)

    def body(t, carry):
        out_ref[:, pl.ds(pl.multiple_of(t * TILE, TILE), TILE)] = ray_sum(
            idx_ref, prod_ref, t, angles, tiles, slots
        )
        return carry

    lax.fori_loop(0, tiles, body, 0)


def forward(packed, column_weight, footprint, volume):
    angles = column_weight.shape[0]
    depth, _, total = volume.shape
    tiles = total // TILE
    banks = footprint.shape[0]
    rows = tiles * angles * depth
    return pl.pallas_call(
        forward_kernel,
        out_shape=jax.ShapeDtypeStruct((angles * depth, total), jnp.float32),
        in_specs=[SMEM, SMEM, VMEM, VMEM],
        out_specs=VMEM,
        scratch_shapes=[
            pltpu.VMEM((rows, TILE), jnp.bfloat16),
            pltpu.VMEM(((banks + 1) * tiles * angles, ROWS, TILE), jnp.float32),
        ],
        compiler_params=pltpu.CompilerParams(vmem_limit_bytes=VMEM_LIMIT),
        name="ray_sums",
    )(packed, column_weight, footprint, volume)


def cone_rows(f, gates):
    depth, width = f.shape
    summed = f
    for h, gate in enumerate(gates, 1):
        zero = jnp.zeros((h, width), jnp.float32)
        beside = jnp.concatenate([zero, f[: depth - h]], axis=0) + jnp.concatenate(
            [f[h:], zero], axis=0
        )
        summed = summed + gate * beside
    return summed


def exchange_kernel(
    count,
    idx_ref,
    w_ref,
    fp_ref,
    vol_ref,
    ext_ref,
    meas_ref,
    ray_ref,
    back_ref,
    sent_ref,
    lhs_ref,
    prod_ref,
    out_buf,
    in_buf,
    total_ref,
    mm_ref,
    rr_ref,
    bb_ref,
    spread_buf,
    send_sem,
    recv_sem,
    send2_sem,
    recv2_sem,
    pair_send,
    pair_recv,
):
    angles = w_ref.shape[0]
    depth = vol_ref.shape[0]
    tiles = vol_ref.shape[2] // TILE
    slots = idx_ref.shape[0] // (angles * tiles)
    half = meas_ref.shape[2] // 2
    per = half // TILE
    k = lax.axis_index("gz")
    other = 1 - k
    me = lax.axis_index("gy") * 2 + k

    def device(d):
        return {"gy": d // 2, "gz": lax.rem(d, 2)}

    barrier = pltpu.get_barrier_semaphore()

    def greet(i, carry):
        d = lax.rem(me + i, count)
        pl.semaphore_signal(barrier, inc=1, device_id=device(d), device_id_type=MESH)
        return carry

    lax.fori_loop(1, count, greet, 0)

    column_sums(w_ref, vol_ref, lhs_ref)
    all_products(lhs_ref, fp_ref, prod_ref, False)

    pl.semaphore_wait(barrier, count - 1)

    mine = pl.ds(pl.multiple_of(k * half, half), half)
    theirs = pl.ds(pl.multiple_of(other * half, half), half)

    def pair(n, src, dst):
        return pltpu.make_async_remote_copy(
            src_ref=src,
            dst_ref=dst,
            send_sem=pair_send.at[n],
            recv_sem=pair_recv.at[n],
            device_id={"gz": other},
            device_id_type=MESH,
        )

    pair_m = pair(0, meas_ref.at[:, :, theirs], mm_ref.at[k])
    pair_r = pair(1, ray_ref.at[:, :, theirs], rr_ref.at[k])
    pair_m.start()
    pair_r.start()
    mm_ref[k] = meas_ref[:, :, mine]
    rr_ref[k] = ray_ref[:, :, mine]

    def scatter_copy(d, slot):
        return pltpu.make_async_remote_copy(
            src_ref=out_buf.at[d],
            dst_ref=in_buf.at[slot],
            send_sem=send_sem.at[d],
            recv_sem=recv_sem.at[slot],
            device_id=device(d),
            device_id_type=MESH,
        )

    def block(d):
        return jnp.concatenate(
            [ray_sum(idx_ref, prod_ref, d * per + h, angles, tiles, slots) for h in range(per)],
            axis=1,
        )

    def project(i, carry):
        d = lax.rem(me + i, count)
        out_buf[d] = block(d).astype(jnp.bfloat16)
        scatter_copy(d, me).start()
        return carry

    lax.fori_loop(1, count, project, 0)
    total_ref[other] = jnp.zeros(total_ref.shape[1:], jnp.float32)
    total_ref[k] = block(me)

    def collect(i, carry):
        s = lax.rem(me + count - i, count)
        scatter_copy(s, s).wait_recv()
        row = lax.rem(s, 2)
        total_ref[row] = total_ref[row] + in_buf[s].astype(jnp.float32)
        return carry

    lax.fori_loop(1, count, collect, 0)

    pair_m.wait_recv()
    pair_r.wait_recv()
    lows, highs = [], []
    for a in range(angles):
        at = slice(a * depth, (a + 1) * depth)
        ext = ext_ref[a : a + 1, mine]
        gates = [jnp.where(ext >= h, c, 0.0) for h, c in enumerate(CONE_WEIGHTS, 1)]
        projected = jnp.concatenate([total_ref[0, at], total_ref[1, at]], axis=0)
        measured = jnp.concatenate([mm_ref[0, a], mm_ref[1, a]], axis=0)
        ray = jnp.concatenate([rr_ref[0, a], rr_ref[1, a]], axis=0)
        rows = cone_rows((measured - cone_rows(projected, gates)) / ray, gates)
        bb_ref[0, a] = rows[:depth]
        bb_ref[1, a] = rows[depth:]
        lows.append(rows[:depth])
        highs.append(rows[depth:])
    spread_buf[0] = jnp.concatenate(lows, axis=0).astype(jnp.bfloat16)
    spread_buf[1] = jnp.concatenate(highs, axis=0).astype(jnp.bfloat16)

    def gather_copy(d, slot):
        return pltpu.make_async_remote_copy(
            src_ref=spread_buf.at[lax.rem(d, 2)],
            dst_ref=sent_ref.at[slot],
            send_sem=send2_sem.at[d],
            recv_sem=recv2_sem.at[slot],
            device_id=device(d),
            device_id_type=MESH,
        )

    def gather_start(i, carry):
        gather_copy(lax.rem(me + i, count), me).start()
        return carry

    lax.fori_loop(1, count, gather_start, 0)
    pair_b = pair(2, bb_ref.at[other], back_ref.at[:, :, mine])
    pair_b.start()
    back_ref[:, :, mine] = bb_ref[k]
    sent_ref[me] = spread_buf[k]

    def finish(i, carry):
        s = lax.rem(me + count - i, count)
        gather_copy(s, s).wait_recv()
        return carry

    lax.fori_loop(1, count, finish, 0)

    def drain(i, carry):
        d = lax.rem(me + i, count)
        scatter_copy(d, me).wait_send()
        gather_copy(d, me).wait_send()
        return carry

    lax.fori_loop(1, count, drain, 0)
    pair_b.wait_recv()
    pair_m.wait_send()
    pair_r.wait_send()
    pair_b.wait_send()


def exchange(count, packed, column_weight, footprint, volume, extent, measured, ray):
    angles = column_weight.shape[0]
    depth, _, total = volume.shape
    tiles = total // TILE
    banks = footprint.shape[0]
    m = angles * depth
    half = measured.shape[2] // 2
    pieces = (2, angles, depth, half)
    return pl.pallas_call(
        functools.partial(exchange_kernel, count),
        out_shape=(
            jax.ShapeDtypeStruct(measured.shape, jnp.float32),
            jax.ShapeDtypeStruct((count, m, half), jnp.bfloat16),
        ),
        in_specs=[SMEM, SMEM, VMEM, VMEM, VMEM, VMEM, VMEM],
        out_specs=(VMEM, VMEM),
        scratch_shapes=[
            pltpu.VMEM((tiles * m, TILE), jnp.bfloat16),
            pltpu.VMEM(((banks + 1) * tiles * angles, ROWS, TILE), jnp.float32),
            pltpu.VMEM((count, m, half), jnp.bfloat16),
            pltpu.VMEM((count, m, half), jnp.bfloat16),
            pltpu.VMEM((2, m, half), jnp.float32),
            pltpu.VMEM(pieces, jnp.float32),
            pltpu.VMEM(pieces, jnp.float32),
            pltpu.VMEM(pieces, jnp.float32),
            pltpu.VMEM((2, m, half), jnp.bfloat16),
            pltpu.SemaphoreType.DMA((count,)),
            pltpu.SemaphoreType.DMA((count,)),
            pltpu.SemaphoreType.DMA((count,)),
            pltpu.SemaphoreType.DMA((count,)),
            pltpu.SemaphoreType.DMA((3,)),
            pltpu.SemaphoreType.DMA((3,)),
        ],
        compiler_params=pltpu.CompilerParams(
            collective_id=0, has_side_effects=True, vmem_limit_bytes=VMEM_LIMIT
        ),
        name="project_and_exchange",
    )(packed, column_weight, footprint, volume, extent, measured, ray)


def shards(
    volume,
    column_weight,
    tile_xblock,
    tile_bank,
    tile_count,
    footprint,
    cone_extent,
    measured,
    ray_length,
):
    angles = column_weight.shape[0]
    depth, _, total = volume.shape
    packed = packed_slots(tile_xblock, tile_bank, tile_count, footprint.shape[0])
    half = measured.shape[2] // 2
    if lax.axis_size("gz") == 2 and half % TILE == 0:
        count = 2 * lax.axis_size("gy")
        back_rows, sent = exchange(
            count, packed, column_weight, footprint, volume, cone_extent, measured, ray_length
        )
        new_volume = back(packed, column_weight, sent, footprint, volume)
    else:
        partial = forward(packed, column_weight, footprint, volume).reshape(angles, depth, total)
        owned = lax.psum_scatter(partial, "gy", scatter_dimension=2, tiled=True)
        predicted = cone_across(owned, cone_extent)
        back_rows = cone_across((measured - predicted) / ray_length, cone_extent)
        sent = lax.all_gather(back_rows.astype(jnp.bfloat16), "gy", axis=2, tiled=True)
        new_volume = back(
            packed, column_weight, sent.reshape(1, angles * depth, total), footprint, volume
        )
    return new_volume, back_rows


def solution(mesh):
    in_specs = (
        P(("parts", "gz"), "gy", None),
        P("parts", "gy"),
        P("parts", "gy", None, None),
        P("parts", "gy", None, None),
        P("parts", "gy", None),
        P(),
        P("parts", "gy"),
        P("parts", "gz", "gy"),
        P("parts", "gz", "gy"),
    )
    out_specs = (P(("parts", "gz"), "gy", None), P("parts", "gz", "gy"))
    return jax.shard_map(shards, mesh=mesh, in_specs=in_specs, out_specs=out_specs, check_vma=False)
```

```python
import functools

import jax
import jax.numpy as jnp
from jax import lax
from jax.experimental import pallas as pl
from jax.experimental.pallas import tpu as pltpu
from jax.sharding import PartitionSpec as P

TILE = 128
ROWS = 8
CONE_WEIGHTS = (0.45, 0.3, 0.2, 0.12)
VMEM_LIMIT = 48 * 2**20
MESH = pl.DeviceIdType.MESH


def extended(cells, axis, dim, width):
    count = lax.axis_size(axis)
    ends = count - 1
    head = lax.slice_in_dim(cells, 0, width, axis=dim)
    tail = lax.slice_in_dim(cells, cells.shape[dim] - width, cells.shape[dim], axis=dim)
    return jnp.concatenate(
        [
            lax.ppermute(tail, axis, [(i, (i + 1) % count) for i in range(ends)]),
            cells,
            lax.ppermute(head, axis, [((i + 1) % count, i) for i in range(ends)]),
        ],
        axis=dim,
    )


def cone_across(signal, extent):
    spread = len(CONE_WEIGHTS)
    depth = signal.shape[1]
    padded = extended(signal, "gz", 1, spread)
    summed = signal
    for offset in range(1, spread + 1):
        gating = (extent >= offset).astype(jnp.float32)[:, None, :]
        beside = (
            padded[:, spread - offset : spread - offset + depth]
            + padded[:, spread + offset : spread + offset + depth]
        )
        summed = summed + CONE_WEIGHTS[offset - 1] * gating * beside
    return summed


def weight_matrix(w_ref, shape, angle_z, z_col):
    angles, cols = w_ref.shape
    a, z = angle_z
    zz, c = z_col
    key = a * cols + c
    out = jnp.zeros(shape, jnp.float32)
    for an in range(angles):
        for cn in range(cols):
            out = jnp.where(key == an * cols + cn, w_ref[an, cn], out)
    return jnp.where(z == zz, out, 0.0)


def split_part(value, part):
    high = value.astype(jnp.bfloat16).astype(jnp.float32)
    rest = value - high
    mid = rest.astype(jnp.bfloat16).astype(jnp.float32)
    return jnp.where(part == 0, high, jnp.where(part == 1, mid, rest - mid)).astype(jnp.bfloat16)


def column_sums(w_ref, vol_ref, lhs_ref):
    angles, cols = w_ref.shape
    depth, _, total = vol_ref.shape
    m = angles * depth
    shape = (3 * m, depth * cols)
    row = lax.broadcasted_iota(jnp.int32, shape, 0)
    col = lax.broadcasted_iota(jnp.int32, shape, 1)
    zb = depth.bit_length() - 1
    cb = cols.bit_length() - 1
    inner = row & (m - 1)
    w = weight_matrix(
        w_ref, shape, (inner >> zb, inner & (depth - 1)), (col >> cb, col & (cols - 1))
    )
    w3 = split_part(w, row >> (m.bit_length() - 1))
    step = 4 * TILE

    def body(i, carry):
        at = pl.ds(pl.multiple_of(i * step, step), step)
        v = jnp.concatenate([vol_ref[z, :, at].astype(jnp.float32) for z in range(depth)], axis=0)
        r = jnp.dot(w3, v.astype(jnp.bfloat16), preferred_element_type=jnp.float32)
        r = (r[:m] + (r[m : 2 * m] + r[2 * m :])).astype(jnp.bfloat16)
        for k in range(4):
            lhs_ref[pl.ds(pl.multiple_of((i * 4 + k) * m, m), m), :] = r[:, k * TILE : (k + 1) * TILE]
        return carry

    lax.fori_loop(0, total // step, body, 0)


def all_products(lhs_ref, fp_ref, prod_ref, transposed):
    banks = fp_ref.shape[0]
    total = lhs_ref.shape[0]
    blocks = total // ROWS
    chunk = 256
    prod_ref[pl.ds(banks * blocks, blocks)] = jnp.zeros((blocks, ROWS, TILE), jnp.float32)

    def body(i, carry):
        b = 2 * i
        if transposed:
            f = jnp.concatenate([fp_ref[b], fp_ref[b + 1]], axis=0)
            dims = (((1,), (1,)), ((), ()))
        else:
            f = jnp.concatenate([fp_ref[b], fp_ref[b + 1]], axis=1)
            dims = (((1,), (0,)), ((), ()))
        for k in range(total // chunk):
            p = lax.dot_general(
                lhs_ref[k * chunk : (k + 1) * chunk, :], f, dims, preferred_element_type=jnp.float32
            )
            n = chunk // ROWS
            for h in range(2):
                prod_ref[pl.ds((b + h) * blocks + k * n, n)] = p[
                    :, h * TILE : (h + 1) * TILE
                ].reshape(n, ROWS, TILE)
        return carry

    lax.fori_loop(0, banks // 2, body, 0)


def ray_sum(idx_ref, prod_ref, t, angles, tiles, slots):
    parts = []
    for a in range(angles):
        terms = [prod_ref[idx_ref[a * tiles + t, s]] for s in range(slots)]
        while len(terms) > 1:
            terms = [sum(terms[i : i + 2][1:], terms[i]) for i in range(0, len(terms), 2)]
        parts.append(terms[0])
    return jnp.concatenate(parts, axis=0)


def packed_slots(xblock, bank, count, banks):
    angles, _, tiles, slots = xblock.shape
    used = jnp.arange(slots)[None, None, :] < count[:, 0, :, None]
    b = jnp.where(used, bank[:, 0], banks)
    angle = jnp.arange(angles, dtype=jnp.int32)[:, None, None]
    return (b * (tiles * angles) + xblock[:, 0] * angles + angle).reshape(-1, slots)


def back_kernel(
    slots,
    table_ref,
    w_ref,
    sent_ref,
    fp_ref,
    vol_ref,
    result_ref,
    lhs_ref,
    prod_ref,
    idx_ref,
    out_ref,
    idx_sem,
    out_sem,
    *acc_refs,
):
    table = pltpu.make_async_copy(table_ref, idx_ref, idx_sem)
    table.start()
    angles, cols = w_ref.shape
    depth, _, total = vol_ref.shape
    tiles = total // TILE
    m = angles * depth
    per = sent_ref.shape[2] // TILE
    for t in range(tiles):
        lhs_ref[t * m : (t + 1) * m, :] = sent_ref[t // per, :, (t % per) * TILE : (t % per + 1) * TILE]
    all_products(lhs_ref, fp_ref, prod_ref, True)
    for acc in acc_refs:
        acc[...] = jnp.zeros_like(acc)
    mask = tiles * angles - 1
    table.wait()

    def body(t, carry):
        for s in range(slots):
            for a in range(angles):
                packed = idx_ref[a * tiles + t, s]
                low = packed & mask
                x = low >> (angles.bit_length() - 1)
                acc_refs[a][x] += prod_ref[packed - low + (t * angles + a)]
        return carry

    lax.fori_loop(0, tiles, body, 0)

    shape = (depth * cols, 3 * m)
    row = lax.broadcasted_iota(jnp.int32, shape, 0)
    col = lax.broadcasted_iota(jnp.int32, shape, 1)
    zb = depth.bit_length() - 1
    cb = cols.bit_length() - 1
    inner = col & (m - 1)
    for extra in (1, 2):
        inner = jnp.where(col >= extra * m, (col - extra * m) & (m - 1), inner)
    w = weight_matrix(
        w_ref, shape, (inner >> zb, inner & (depth - 1)), (row >> cb, row & (cols - 1))
    )
    w3 = split_part(w, jnp.where(col >= 2 * m, 1, 0))
    step = 4

    def piece(i):
        at = pl.ds(pl.multiple_of(i * step * TILE, step * TILE), step * TILE)
        return pltpu.make_async_copy(out_ref.at[:, :, at], result_ref.at[:, :, at], out_sem.at[i])

    def finish(i, carry):
        s = jnp.concatenate(
            [
                jnp.concatenate([acc_refs[a][i * step + k] for k in range(step)], axis=1)
                for a in range(angles)
            ],
            axis=0,
        )
        high = s.astype(jnp.bfloat16)
        low = (s - high.astype(jnp.float32)).astype(jnp.bfloat16)
        change = jnp.dot(
            w3, jnp.concatenate([high, low, high], axis=0), preferred_element_type=jnp.float32
        )
        at = pl.ds(pl.multiple_of(i * step * TILE, step * TILE), step * TILE)
        for z in range(depth):
            fresh = vol_ref[z, :, at].astype(jnp.float32) + change[z * cols : (z + 1) * cols]
            out_ref[z, :, at] = jnp.maximum(fresh, 0.0).astype(jnp.bfloat16)
        piece(i).start()
        return carry

    lax.fori_loop(0, tiles // step, finish, 0)
    for i in range(tiles // step):
        piece(i).wait()


SMEM = pl.BlockSpec(memory_space=pltpu.SMEM)
VMEM = pl.BlockSpec(memory_space=pltpu.VMEM)
HBM = pl.BlockSpec(memory_space=pltpu.HBM)


def back(slots, packed, column_weight, sent, footprint, volume):
    angles = column_weight.shape[0]
    depth, _, total = volume.shape
    tiles = total // TILE
    banks = footprint.shape[0]
    rows = tiles * angles * depth
    return pl.pallas_call(
        functools.partial(back_kernel, slots),
        out_shape=jax.ShapeDtypeStruct(volume.shape, jnp.bfloat16),
        in_specs=[HBM, SMEM, VMEM, VMEM, VMEM],
        out_specs=HBM,
        scratch_shapes=[
            pltpu.VMEM((rows, TILE), jnp.bfloat16),
            pltpu.VMEM(((banks + 1) * tiles * angles, ROWS, TILE), jnp.float32),
            pltpu.SMEM(packed.shape, jnp.int32),
            pltpu.VMEM(volume.shape, jnp.bfloat16),
            pltpu.SemaphoreType.DMA,
            pltpu.SemaphoreType.DMA((tiles // 4,)),
        ]
        + [pltpu.VMEM((tiles, ROWS, TILE), jnp.float32) for _ in range(angles)],
        compiler_params=pltpu.CompilerParams(vmem_limit_bytes=VMEM_LIMIT),
        name="back_spread",
    )(packed, column_weight, sent, footprint, volume)


def forward_kernel(idx_ref, w_ref, fp_ref, vol_ref, out_ref, lhs_ref, prod_ref):
    angles = w_ref.shape[0]
    tiles = vol_ref.shape[2] // TILE
    slots = idx_ref.shape[1]
    column_sums(w_ref, vol_ref, lhs_ref)
    all_products(lhs_ref, fp_ref, prod_ref, False)

    def body(t, carry):
        out_ref[:, pl.ds(pl.multiple_of(t * TILE, TILE), TILE)] = ray_sum(
            idx_ref, prod_ref, t, angles, tiles, slots
        )
        return carry

    lax.fori_loop(0, tiles, body, 0)


def forward(packed, column_weight, footprint, volume):
    angles = column_weight.shape[0]
    depth, _, total = volume.shape
    tiles = total // TILE
    banks = footprint.shape[0]
    rows = tiles * angles * depth
    return pl.pallas_call(
        forward_kernel,
        out_shape=jax.ShapeDtypeStruct((angles * depth, total), jnp.float32),
        in_specs=[SMEM, SMEM, VMEM, VMEM],
        out_specs=VMEM,
        scratch_shapes=[
            pltpu.VMEM((rows, TILE), jnp.bfloat16),
            pltpu.VMEM(((banks + 1) * tiles * angles, ROWS, TILE), jnp.float32),
        ],
        compiler_params=pltpu.CompilerParams(vmem_limit_bytes=VMEM_LIMIT),
        name="ray_sums",
    )(packed, column_weight, footprint, volume)


def cone_rows(f, gates):
    depth, width = f.shape
    summed = f
    for h, gate in enumerate(gates, 1):
        zero = jnp.zeros((h, width), jnp.float32)
        beside = jnp.concatenate([zero, f[: depth - h]], axis=0) + jnp.concatenate(
            [f[h:], zero], axis=0
        )
        summed = summed + gate * beside
    return summed


def exchange_kernel(
    count,
    w_ref,
    xblock_hbm,
    bank_hbm,
    filled_hbm,
    fp_hbm,
    vol_hbm,
    ext_hbm,
    meas_hbm,
    ray_hbm,
    back_ref,
    sent_ref,
    table_hbm,
    xblock_ref,
    bank_ref,
    filled_ref,
    fp_ref,
    vol_ref,
    ext_ref,
    meas_ref,
    ray_ref,
    table_ref,
    idx_ref,
    load_sem,
    lhs_ref,
    prod_ref,
    out_buf,
    in_buf,
    total_ref,
    mm_ref,
    rr_ref,
    bb_ref,
    spread_buf,
    send_sem,
    recv_sem,
    send2_sem,
    recv2_sem,
    pair_send,
    pair_recv,
):
    angles = w_ref.shape[0]
    depth = vol_ref.shape[0]
    tiles = vol_ref.shape[2] // TILE
    slots = xblock_ref.shape[3]
    banks = fp_ref.shape[0]
    half = meas_ref.shape[2] // 2
    per = half // TILE
    k = lax.axis_index("gz")
    other = 1 - k
    me = lax.axis_index("gy") * 2 + k

    def device(d):
        return {"gy": d // 2, "gz": lax.rem(d, 2)}

    loads = [
        pltpu.make_async_copy(src, dst, load_sem.at[n])
        for n, (src, dst) in enumerate(
            (
                (vol_hbm, vol_ref),
                (fp_hbm, fp_ref),
                (xblock_hbm, xblock_ref),
                (bank_hbm, bank_ref),
                (filled_hbm, filled_ref),
                (ext_hbm, ext_ref),
                (meas_hbm, meas_ref),
                (ray_hbm, ray_ref),
            )
        )
    ]
    for load in loads:
        load.start()
    barrier = pltpu.get_barrier_semaphore()

    def greet(i, carry):
        d = lax.rem(me + i, count)
        pl.semaphore_signal(barrier, inc=1, device_id=device(d), device_id_type=MESH)
        return carry

    lax.fori_loop(1, count, greet, 0)

    for load in loads[2:5]:
        load.wait()
    table_ref[...] = jnp.zeros_like(table_ref)
    lane = lax.broadcasted_iota(jnp.int32, (tiles, slots), 1)
    square = (tiles, tiles)
    eye = lax.broadcasted_iota(jnp.int32, square, 0) == lax.broadcasted_iota(jnp.int32, square, 1)
    for a in range(angles):
        filled = jnp.broadcast_to(filled_ref[a].astype(jnp.float32), square)
        filled = jnp.sum(jnp.where(eye, filled, 0.0), axis=1, keepdims=True)
        bank = jnp.where(lane.astype(jnp.float32) < filled, bank_ref[a, 0], banks)
        table_ref[a * tiles : (a + 1) * tiles, :slots] = (
            bank * (tiles * angles) + xblock_ref[a, 0] * angles + a
        )
    tables = (
        pltpu.make_async_copy(table_ref, idx_ref, load_sem.at[len(loads)]),
        pltpu.make_async_copy(table_ref, table_hbm, load_sem.at[len(loads) + 1]),
    )
    for table in tables:
        table.start()

    loads[0].wait()
    column_sums(w_ref, vol_ref, lhs_ref)
    loads[1].wait()
    all_products(lhs_ref, fp_ref, prod_ref, False)
    for waited in loads[5:] + list(tables):
        waited.wait()

    pl.semaphore_wait(barrier, count - 1)

    mine = pl.ds(pl.multiple_of(k * half, half), half)
    theirs = pl.ds(pl.multiple_of(other * half, half), half)

    def pair(n, src, dst):
        return pltpu.make_async_remote_copy(
            src_ref=src,
            dst_ref=dst,
            send_sem=pair_send.at[n],
            recv_sem=pair_recv.at[n],
            device_id={"gz": other},
            device_id_type=MESH,
        )

    pair_m = pair(0, meas_ref.at[:, :, theirs], mm_ref.at[k])
    pair_r = pair(1, ray_ref.at[:, :, theirs], rr_ref.at[k])
    pair_m.start()
    pair_r.start()
    mm_ref[k] = meas_ref[:, :, mine]
    rr_ref[k] = ray_ref[:, :, mine]

    def scatter_copy(d, slot):
        return pltpu.make_async_remote_copy(
            src_ref=out_buf.at[d],
            dst_ref=in_buf.at[slot],
            send_sem=send_sem.at[d],
            recv_sem=recv_sem.at[slot],
            device_id=device(d),
            device_id_type=MESH,
        )

    def block(d):
        return jnp.concatenate(
            [ray_sum(idx_ref, prod_ref, d * per + h, angles, tiles, slots) for h in range(per)],
            axis=1,
        )

    def project(i, carry):
        d = lax.rem(me + i, count)
        out_buf[d] = block(d).astype(jnp.bfloat16)
        scatter_copy(d, me).start()
        return carry

    lax.fori_loop(1, count, project, 0)
    total_ref[other] = jnp.zeros(total_ref.shape[1:], jnp.float32)
    total_ref[k] = block(me)

    def collect(i, carry):
        s = lax.rem(me + count - i, count)
        scatter_copy(s, s).wait_recv()
        row = lax.rem(s, 2)
        total_ref[row] = total_ref[row] + in_buf[s].astype(jnp.float32)
        return carry

    lax.fori_loop(1, count, collect, 0)

    pair_m.wait_recv()
    pair_r.wait_recv()
    lows, highs = [], []
    for a in range(angles):
        at = slice(a * depth, (a + 1) * depth)
        ext = ext_ref[a : a + 1, mine]
        gates = [jnp.where(ext >= h, c, 0.0) for h, c in enumerate(CONE_WEIGHTS, 1)]
        projected = jnp.concatenate([total_ref[0, at], total_ref[1, at]], axis=0)
        measured = jnp.concatenate([mm_ref[0, a], mm_ref[1, a]], axis=0)
        ray = jnp.concatenate([rr_ref[0, a], rr_ref[1, a]], axis=0)
        rows = cone_rows((measured - cone_rows(projected, gates)) / ray, gates)
        bb_ref[0, a] = rows[:depth]
        bb_ref[1, a] = rows[depth:]
        lows.append(rows[:depth])
        highs.append(rows[depth:])
    spread_buf[0] = jnp.concatenate(lows, axis=0).astype(jnp.bfloat16)
    spread_buf[1] = jnp.concatenate(highs, axis=0).astype(jnp.bfloat16)

    def gather_copy(d, slot):
        return pltpu.make_async_remote_copy(
            src_ref=spread_buf.at[lax.rem(d, 2)],
            dst_ref=sent_ref.at[slot],
            send_sem=send2_sem.at[d],
            recv_sem=recv2_sem.at[slot],
            device_id=device(d),
            device_id_type=MESH,
        )

    def gather_start(i, carry):
        gather_copy(lax.rem(me + i, count), me).start()
        return carry

    lax.fori_loop(1, count, gather_start, 0)
    pair_b = pair(2, bb_ref.at[other], back_ref.at[:, :, mine])
    pair_b.start()
    back_ref[:, :, mine] = bb_ref[k]
    sent_ref[me] = spread_buf[k]

    def finish(i, carry):
        s = lax.rem(me + count - i, count)
        gather_copy(s, s).wait_recv()
        return carry

    lax.fori_loop(1, count, finish, 0)

    def drain(i, carry):
        d = lax.rem(me + i, count)
        scatter_copy(d, me).wait_send()
        gather_copy(d, me).wait_send()
        return carry

    lax.fori_loop(1, count, drain, 0)
    pair_b.wait_recv()
    pair_m.wait_send()
    pair_r.wait_send()
    pair_b.wait_send()


def exchange(
    count, column_weight, xblock, bank, filled, footprint, volume, extent, measured, ray
):
    operands = (xblock, bank, filled, footprint, volume, extent, measured, ray)
    angles = column_weight.shape[0]
    depth, _, total = volume.shape
    tiles = total // TILE
    banks = footprint.shape[0]
    m = angles * depth
    half = measured.shape[2] // 2
    pieces = (2, angles, depth, half)
    return pl.pallas_call(
        functools.partial(exchange_kernel, count),
        out_shape=(
            jax.ShapeDtypeStruct(measured.shape, jnp.float32),
            jax.ShapeDtypeStruct((count, m, half), jnp.bfloat16),
            jax.ShapeDtypeStruct((angles * tiles, TILE), jnp.int32),
        ),
        in_specs=[SMEM] + [HBM] * len(operands),
        out_specs=(VMEM, VMEM, HBM),
        scratch_shapes=[pltpu.VMEM(x.shape, x.dtype) for x in operands]
        + [
            pltpu.VMEM((angles * tiles, TILE), jnp.int32),
            pltpu.SMEM((angles * tiles, TILE), jnp.int32),
            pltpu.SemaphoreType.DMA((len(operands) + 2,)),
            pltpu.VMEM((tiles * m, TILE), jnp.bfloat16),
            pltpu.VMEM(((banks + 1) * tiles * angles, ROWS, TILE), jnp.float32),
            pltpu.VMEM((count, m, half), jnp.bfloat16),
            pltpu.VMEM((count, m, half), jnp.bfloat16),
            pltpu.VMEM((2, m, half), jnp.float32),
            pltpu.VMEM(pieces, jnp.float32),
            pltpu.VMEM(pieces, jnp.float32),
            pltpu.VMEM(pieces, jnp.float32),
            pltpu.VMEM((2, m, half), jnp.bfloat16),
            pltpu.SemaphoreType.DMA((count,)),
            pltpu.SemaphoreType.DMA((count,)),
            pltpu.SemaphoreType.DMA((count,)),
            pltpu.SemaphoreType.DMA((count,)),
            pltpu.SemaphoreType.DMA((3,)),
            pltpu.SemaphoreType.DMA((3,)),
        ],
        compiler_params=pltpu.CompilerParams(
            collective_id=0, has_side_effects=True, vmem_limit_bytes=VMEM_LIMIT
        ),
        name="project_and_exchange",
    )(column_weight, *operands)


def shards(
    volume,
    column_weight,
    tile_xblock,
    tile_bank,
    tile_count,
    footprint,
    cone_extent,
    measured,
    ray_length,
):
    angles = column_weight.shape[0]
    depth, _, total = volume.shape
    slots = tile_xblock.shape[3]
    half = measured.shape[2] // 2
    if lax.axis_size("gz") == 2 and half % TILE == 0:
        count = 2 * lax.axis_size("gy")
        back_rows, sent, packed = exchange(
            count,
            column_weight,
            tile_xblock,
            tile_bank,
            tile_count,
            footprint,
            volume,
            cone_extent,
            measured,
            ray_length,
        )
        new_volume = back(slots, packed, column_weight, sent, footprint, volume)
    else:
        packed = packed_slots(tile_xblock, tile_bank, tile_count, footprint.shape[0])
        partial = forward(packed, column_weight, footprint, volume).reshape(angles, depth, total)
        owned = lax.psum_scatter(partial, "gy", scatter_dimension=2, tiled=True)
        predicted = cone_across(owned, cone_extent)
        back_rows = cone_across((measured - predicted) / ray_length, cone_extent)
        sent = lax.all_gather(back_rows.astype(jnp.bfloat16), "gy", axis=2, tiled=True)
        packed = jnp.pad(packed, ((0, 0), (0, TILE - slots)))
        new_volume = back(
            slots, packed, column_weight, sent.reshape(1, angles * depth, total), footprint, volume
        )
    return new_volume, back_rows


def solution(mesh):
    in_specs = (
        P(("parts", "gz"), "gy", None),
        P("parts", "gy"),
        P("parts", "gy", None, None),
        P("parts", "gy", None, None),
        P("parts", "gy", None),
        P(),
        P("parts", "gy"),
        P("parts", "gz", "gy"),
        P("parts", "gz", "gy"),
    )
    out_specs = (P(("parts", "gz"), "gy", None), P("parts", "gz", "gy"))
    return jax.shard_map(shards, mesh=mesh, in_specs=in_specs, out_specs=out_specs, check_vma=False)
```

```python
import functools
import math

import jax
import jax.numpy as jnp
from jax import lax
from jax.experimental import pallas as pl
from jax.experimental.pallas import tpu as pltpu
from jax.sharding import PartitionSpec as P

TILE = 128
ROWS = 8
CONE_WEIGHTS = (0.45, 0.3, 0.2, 0.12)
VMEM_LIMIT = 64 * 2**20 - 2**18
MESH = pl.DeviceIdType.MESH


def extended(cells, axis, dim, width):
    count = lax.axis_size(axis)
    ends = count - 1
    head = lax.slice_in_dim(cells, 0, width, axis=dim)
    tail = lax.slice_in_dim(cells, cells.shape[dim] - width, cells.shape[dim], axis=dim)
    return jnp.concatenate(
        [
            lax.ppermute(tail, axis, [(i, (i + 1) % count) for i in range(ends)]),
            cells,
            lax.ppermute(head, axis, [((i + 1) % count, i) for i in range(ends)]),
        ],
        axis=dim,
    )


def cone_across(signal, extent):
    spread = len(CONE_WEIGHTS)
    depth = signal.shape[1]
    padded = extended(signal, "gz", 1, spread)
    summed = signal
    for offset in range(1, spread + 1):
        gating = (extent >= offset).astype(jnp.float32)[:, None, :]
        beside = (
            padded[:, spread - offset : spread - offset + depth]
            + padded[:, spread + offset : spread + offset + depth]
        )
        summed = summed + CONE_WEIGHTS[offset - 1] * gating * beside
    return summed


def weight_matrix(w_ref, shape, angle_z, z_col):
    angles, cols = w_ref.shape
    a, z = angle_z
    zz, c = z_col
    key = a * cols + c
    out = jnp.zeros(shape, jnp.float32)
    for an in range(angles):
        for cn in range(cols):
            out = jnp.where(key == an * cols + cn, w_ref[an, cn], out)
    return jnp.where(z == zz, out, 0.0)


def split_part(value, part):
    high = value.astype(jnp.bfloat16).astype(jnp.float32)
    rest = value - high
    mid = rest.astype(jnp.bfloat16).astype(jnp.float32)
    return jnp.where(part == 0, high, jnp.where(part == 1, mid, rest - mid)).astype(jnp.bfloat16)


def column_sums(w_ref, vol_ref, lhs_ref):
    angles, cols = w_ref.shape
    depth, _, total = vol_ref.shape
    m = angles * depth
    shape = (3 * m, depth * cols)
    row = lax.broadcasted_iota(jnp.int32, shape, 0)
    col = lax.broadcasted_iota(jnp.int32, shape, 1)
    zb = depth.bit_length() - 1
    cb = cols.bit_length() - 1
    inner = row & (m - 1)
    w = weight_matrix(
        w_ref, shape, (inner >> zb, inner & (depth - 1)), (col >> cb, col & (cols - 1))
    )
    w3 = split_part(w, row >> (m.bit_length() - 1))
    step = 4 * TILE

    def body(i, carry):
        at = pl.ds(pl.multiple_of(i * step, step), step)
        v = jnp.concatenate([vol_ref[z, :, at].astype(jnp.float32) for z in range(depth)], axis=0)
        r = jnp.dot(w3, v.astype(jnp.bfloat16), preferred_element_type=jnp.float32)
        r = (r[:m] + (r[m : 2 * m] + r[2 * m :])).astype(jnp.bfloat16)
        for k in range(4):
            lhs_ref[pl.ds(pl.multiple_of((i * 4 + k) * m, m), m), :] = r[:, k * TILE : (k + 1) * TILE]
        return carry

    lax.fori_loop(0, total // step, body, 0)


def all_products(lhs_ref, fp_ref, prod_ref, transposed):
    banks = fp_ref.shape[0]
    total = lhs_ref.shape[0]
    blocks = total // ROWS
    chunk = 256
    prod_ref[pl.ds(banks * blocks, blocks)] = jnp.zeros((blocks, ROWS, TILE), jnp.float32)

    def body(i, carry):
        b = 2 * i
        if transposed:
            f = jnp.concatenate([fp_ref[b], fp_ref[b + 1]], axis=0)
            dims = (((1,), (1,)), ((), ()))
        else:
            f = jnp.concatenate([fp_ref[b], fp_ref[b + 1]], axis=1)
            dims = (((1,), (0,)), ((), ()))
        for k in range(total // chunk):
            p = lax.dot_general(
                lhs_ref[k * chunk : (k + 1) * chunk, :], f, dims, preferred_element_type=jnp.float32
            )
            n = chunk // ROWS
            for h in range(2):
                prod_ref[pl.ds((b + h) * blocks + k * n, n)] = p[
                    :, h * TILE : (h + 1) * TILE
                ].reshape(n, ROWS, TILE)
        return carry

    lax.fori_loop(0, banks // 2, body, 0)


def ray_sum(idx_ref, prod_ref, t, angles, tiles, slots):
    parts = []
    for a in range(angles):
        terms = [prod_ref[idx_ref[a * slots + s, t]] for s in range(slots)]
        while len(terms) > 1:
            terms = [sum(terms[i : i + 2][1:], terms[i]) for i in range(0, len(terms), 2)]
        parts.append(terms[0])
    return jnp.concatenate(parts, axis=0)


def packed_slots(xblock, bank, count, banks):
    angles, slots, _, tiles = xblock.shape
    used = jnp.arange(slots)[None, :, None, None] < count[:, None]
    b = jnp.where(used, bank, banks)
    angle = jnp.arange(angles, dtype=jnp.int32)[:, None, None, None]
    packed = (b * (tiles * angles) + xblock * angles + angle).reshape(angles * slots, tiles)
    return jnp.pad(packed, ((0, 0), (0, TILE - tiles)))


def back_kernel(
    table_ref,
    w_ref,
    sent_hbm,
    fp_hbm,
    vol_hbm,
    rows_in_ref,
    result_ref,
    rows_out_ref,
    lhs_ref,
    prod_ref,
    fp_ref,
    vol_ref,
    sent_ref,
    idx_ref,
    out_ref,
    load_sem,
    sent_sem,
    out_sem,
    *acc_refs,
):
    sources = sent_hbm.shape[0]
    batches = math.gcd(sources, 4)
    group = sources // batches
    arrivals = []
    for n in range(batches):
        at = pl.ds(n * group, group)
        arrivals.append(
            pltpu.make_async_copy(sent_hbm.at[at], sent_ref.at[at], sent_sem.at[n])
        )
        arrivals[n].start()
    footprints = pltpu.make_async_copy(fp_hbm, fp_ref, load_sem.at[0])
    table = pltpu.make_async_copy(table_ref, idx_ref, load_sem.at[1])
    columns = pltpu.make_async_copy(vol_hbm, vol_ref, load_sem.at[2])
    rows_out = pltpu.make_async_copy(rows_in_ref, rows_out_ref, load_sem.at[3])
    for load in (footprints, table, columns, rows_out):
        load.start()
    angles, cols = w_ref.shape
    depth, _, total = vol_ref.shape
    tiles = total // TILE
    slots = idx_ref.shape[0] // angles
    m = angles * depth
    per = sent_ref.shape[2] // TILE
    for t in range(tiles):
        if t % (per * group) == 0:
            arrivals[t // (per * group)].wait()
        lhs_ref[t * m : (t + 1) * m, :] = sent_ref[t // per, :, (t % per) * TILE : (t % per + 1) * TILE]
    footprints.wait()
    all_products(lhs_ref, fp_ref, prod_ref, True)
    for acc in acc_refs:
        acc[...] = jnp.zeros_like(acc)
    mask = tiles * angles - 1
    table.wait()

    def body(t, carry):
        for s in range(slots):
            for a in range(angles):
                packed = idx_ref[a * slots + s, t]
                low = packed & mask
                x = low >> (angles.bit_length() - 1)
                acc_refs[a][x] += prod_ref[packed - low + (t * angles + a)]
        return carry

    lax.fori_loop(0, tiles, body, 0)

    shape = (depth * cols, 3 * m)
    row = lax.broadcasted_iota(jnp.int32, shape, 0)
    col = lax.broadcasted_iota(jnp.int32, shape, 1)
    zb = depth.bit_length() - 1
    cb = cols.bit_length() - 1
    inner = col & (m - 1)
    for extra in (1, 2):
        inner = jnp.where(col >= extra * m, (col - extra * m) & (m - 1), inner)
    w = weight_matrix(
        w_ref, shape, (inner >> zb, inner & (depth - 1)), (row >> cb, row & (cols - 1))
    )
    w3 = split_part(w, jnp.where(col >= 2 * m, 1, 0))
    step = 4

    columns.wait()

    def piece(i):
        at = pl.ds(pl.multiple_of(i * step * TILE, step * TILE), step * TILE)
        return pltpu.make_async_copy(out_ref.at[:, :, at], result_ref.at[:, :, at], out_sem.at[i])

    def finish(i, carry):
        s = jnp.concatenate(
            [
                jnp.concatenate([acc_refs[a][i * step + k] for k in range(step)], axis=1)
                for a in range(angles)
            ],
            axis=0,
        )
        high = s.astype(jnp.bfloat16)
        low = (s - high.astype(jnp.float32)).astype(jnp.bfloat16)
        change = jnp.dot(
            w3, jnp.concatenate([high, low, high], axis=0), preferred_element_type=jnp.float32
        )
        at = pl.ds(pl.multiple_of(i * step * TILE, step * TILE), step * TILE)
        for z in range(depth):
            fresh = vol_ref[z, :, at].astype(jnp.float32) + change[z * cols : (z + 1) * cols]
            out_ref[z, :, at] = jnp.maximum(fresh, 0.0).astype(jnp.bfloat16)
        piece(i).start()
        return carry

    lax.fori_loop(0, tiles // step, finish, 0)
    for i in range(tiles // step):
        piece(i).wait()
    rows_out.wait()


SMEM = pl.BlockSpec(memory_space=pltpu.SMEM)
VMEM = pl.BlockSpec(memory_space=pltpu.VMEM)
HBM = pl.BlockSpec(memory_space=pltpu.HBM)


def back(packed, column_weight, sent, footprint, volume, back_rows):
    angles = column_weight.shape[0]
    depth, _, total = volume.shape
    tiles = total // TILE
    banks = footprint.shape[0]
    rows = tiles * angles * depth
    return pl.pallas_call(
        back_kernel,
        out_shape=(
            jax.ShapeDtypeStruct(volume.shape, jnp.bfloat16),
            jax.ShapeDtypeStruct(back_rows.shape, jnp.float32),
        ),
        in_specs=[HBM, SMEM, HBM, HBM, HBM, HBM],
        out_specs=(HBM, HBM),
        scratch_shapes=[
            pltpu.VMEM((rows, TILE), jnp.bfloat16),
            pltpu.VMEM(((banks + 1) * tiles * angles, ROWS, TILE), jnp.float32),
            pltpu.VMEM(footprint.shape, jnp.bfloat16),
            pltpu.VMEM(volume.shape, jnp.bfloat16),
            pltpu.VMEM(sent.shape, jnp.bfloat16),
            pltpu.SMEM(packed.shape, jnp.int32),
            pltpu.VMEM(volume.shape, jnp.bfloat16),
            pltpu.SemaphoreType.DMA((4,)),
            pltpu.SemaphoreType.DMA((4,)),
            pltpu.SemaphoreType.DMA((tiles // 4,)),
        ]
        + [pltpu.VMEM((tiles, ROWS, TILE), jnp.float32) for _ in range(angles)],
        compiler_params=pltpu.CompilerParams(vmem_limit_bytes=VMEM_LIMIT),
        name="back_spread",
    )(packed, column_weight, sent, footprint, volume, back_rows)


def forward_kernel(idx_ref, w_ref, fp_ref, vol_ref, out_ref, lhs_ref, prod_ref):
    angles = w_ref.shape[0]
    tiles = vol_ref.shape[2] // TILE
    slots = idx_ref.shape[0] // angles
    column_sums(w_ref, vol_ref, lhs_ref)
    all_products(lhs_ref, fp_ref, prod_ref, False)

    def body(t, carry):
        out_ref[:, pl.ds(pl.multiple_of(t * TILE, TILE), TILE)] = ray_sum(
            idx_ref, prod_ref, t, angles, tiles, slots
        )
        return carry

    lax.fori_loop(0, tiles, body, 0)


def forward(packed, column_weight, footprint, volume):
    angles = column_weight.shape[0]
    depth, _, total = volume.shape
    tiles = total // TILE
    banks = footprint.shape[0]
    rows = tiles * angles * depth
    return pl.pallas_call(
        forward_kernel,
        out_shape=jax.ShapeDtypeStruct((angles * depth, total), jnp.float32),
        in_specs=[SMEM, SMEM, VMEM, VMEM],
        out_specs=VMEM,
        scratch_shapes=[
            pltpu.VMEM((rows, TILE), jnp.bfloat16),
            pltpu.VMEM(((banks + 1) * tiles * angles, ROWS, TILE), jnp.float32),
        ],
        compiler_params=pltpu.CompilerParams(vmem_limit_bytes=VMEM_LIMIT),
        name="ray_sums",
    )(packed, column_weight, footprint, volume)


def cone_rows(f, gates):
    depth, width = f.shape
    summed = f
    for h, gate in enumerate(gates, 1):
        zero = jnp.zeros((h, width), jnp.float32)
        beside = jnp.concatenate([zero, f[: depth - h]], axis=0) + jnp.concatenate(
            [f[h:], zero], axis=0
        )
        summed = summed + gate * beside
    return summed


def exchange_kernel(
    count,
    w_ref,
    xblock_hbm,
    bank_hbm,
    filled_hbm,
    fp_hbm,
    vol_hbm,
    ext_hbm,
    meas_hbm,
    ray_hbm,
    back_ref,
    sent_ref,
    table_hbm,
    xblock_ref,
    bank_ref,
    filled_ref,
    fp_ref,
    vol_ref,
    ext_ref,
    meas_ref,
    ray_ref,
    table_ref,
    idx_ref,
    load_sem,
    lhs_ref,
    prod_ref,
    out_buf,
    in_buf,
    total_ref,
    mm_ref,
    rr_ref,
    bb_ref,
    spread_buf,
    send_sem,
    recv_sem,
    send2_sem,
    recv2_sem,
    pair_send,
    pair_recv,
):
    angles = w_ref.shape[0]
    depth = vol_ref.shape[0]
    tiles = vol_ref.shape[2] // TILE
    slots = xblock_ref.shape[1]
    banks = fp_ref.shape[0]
    half = meas_ref.shape[2] // 2
    per = half // TILE
    k = lax.axis_index("gz")
    other = 1 - k
    me = lax.axis_index("gy") * 2 + k

    def device(d):
        return {"gy": d // 2, "gz": lax.rem(d, 2)}

    loads = [
        pltpu.make_async_copy(src, dst, load_sem.at[n])
        for n, (src, dst) in enumerate(
            (
                (vol_hbm, vol_ref),
                (fp_hbm, fp_ref),
                (xblock_hbm, xblock_ref),
                (bank_hbm, bank_ref),
                (filled_hbm, filled_ref),
                (ext_hbm, ext_ref),
                (meas_hbm, meas_ref),
                (ray_hbm, ray_ref),
            )
        )
    ]
    for load in loads:
        load.start()
    barrier = pltpu.get_barrier_semaphore()

    def greet(i, carry):
        d = lax.rem(me + i, count)
        pl.semaphore_signal(barrier, inc=1, device_id=device(d), device_id_type=MESH)
        return carry

    lax.fori_loop(1, count, greet, 0)

    for load in loads[2:5]:
        load.wait()
    table_ref[...] = jnp.zeros_like(table_ref)
    for a in range(angles):
        for n in range(slots):
            bank = jnp.where(n < filled_ref[a], bank_ref[a, n], banks)
            table_ref[a * slots + n : a * slots + n + 1, :tiles] = (
                bank * (tiles * angles) + xblock_ref[a, n] * angles + a
            )
    tables = (
        pltpu.make_async_copy(table_ref, idx_ref, load_sem.at[len(loads)]),
        pltpu.make_async_copy(table_ref, table_hbm, load_sem.at[len(loads) + 1]),
    )
    for table in tables:
        table.start()

    loads[0].wait()
    column_sums(w_ref, vol_ref, lhs_ref)
    loads[1].wait()
    all_products(lhs_ref, fp_ref, prod_ref, False)
    for waited in loads[5:] + list(tables):
        waited.wait()

    pl.semaphore_wait(barrier, count - 1)

    mine = pl.ds(pl.multiple_of(k * half, half), half)
    theirs = pl.ds(pl.multiple_of(other * half, half), half)

    def pair(n, src, dst):
        return pltpu.make_async_remote_copy(
            src_ref=src,
            dst_ref=dst,
            send_sem=pair_send.at[n],
            recv_sem=pair_recv.at[n],
            device_id={"gz": other},
            device_id_type=MESH,
        )

    pair_m = pair(0, meas_ref.at[:, :, theirs], mm_ref.at[k])
    pair_r = pair(1, ray_ref.at[:, :, theirs], rr_ref.at[k])
    pair_m.start()
    pair_r.start()
    mm_ref[k] = meas_ref[:, :, mine]
    rr_ref[k] = ray_ref[:, :, mine]

    def scatter_copy(d, slot):
        return pltpu.make_async_remote_copy(
            src_ref=out_buf.at[d],
            dst_ref=in_buf.at[slot],
            send_sem=send_sem.at[d],
            recv_sem=recv_sem.at[slot],
            device_id=device(d),
            device_id_type=MESH,
        )

    def block(d):
        return jnp.concatenate(
            [ray_sum(idx_ref, prod_ref, d * per + h, angles, tiles, slots) for h in range(per)],
            axis=1,
        )

    def project(i, carry):
        d = lax.rem(me + i, count)
        out_buf[d] = block(d).astype(jnp.bfloat16)
        scatter_copy(d, me).start()
        return carry

    lax.fori_loop(1, count, project, 0)
    total_ref[other] = jnp.zeros(total_ref.shape[1:], jnp.float32)
    total_ref[k] = block(me)

    def collect(i, carry):
        s = lax.rem(me + count - i, count)
        scatter_copy(s, s).wait_recv()
        row = lax.rem(s, 2)
        total_ref[row] = total_ref[row] + in_buf[s].astype(jnp.float32)
        return carry

    lax.fori_loop(1, count, collect, 0)

    pair_m.wait_recv()
    pair_r.wait_recv()
    lows, highs = [], []
    for a in range(angles):
        at = slice(a * depth, (a + 1) * depth)
        ext = ext_ref[a : a + 1, mine]
        gates = [jnp.where(ext >= h, c, 0.0) for h, c in enumerate(CONE_WEIGHTS, 1)]
        projected = jnp.concatenate([total_ref[0, at], total_ref[1, at]], axis=0)
        measured = jnp.concatenate([mm_ref[0, a], mm_ref[1, a]], axis=0)
        ray = jnp.concatenate([rr_ref[0, a], rr_ref[1, a]], axis=0)
        rows = cone_rows((measured - cone_rows(projected, gates)) / ray, gates)
        bb_ref[0, a] = rows[:depth]
        bb_ref[1, a] = rows[depth:]
        lows.append(rows[:depth])
        highs.append(rows[depth:])
    spread_buf[0] = jnp.concatenate(lows, axis=0).astype(jnp.bfloat16)
    spread_buf[1] = jnp.concatenate(highs, axis=0).astype(jnp.bfloat16)

    def gather_copy(d, slot):
        return pltpu.make_async_remote_copy(
            src_ref=spread_buf.at[lax.rem(d, 2)],
            dst_ref=sent_ref.at[slot],
            send_sem=send2_sem.at[d],
            recv_sem=recv2_sem.at[slot],
            device_id=device(d),
            device_id_type=MESH,
        )

    def gather_start(i, carry):
        gather_copy(lax.rem(me + i, count), me).start()
        return carry

    lax.fori_loop(1, count, gather_start, 0)
    pair_b = pair(2, bb_ref.at[other], back_ref.at[:, :, mine])
    pair_b.start()
    kept = (
        pltpu.make_async_copy(bb_ref.at[k], back_ref.at[:, :, mine], load_sem.at[0]),
        pltpu.make_async_copy(spread_buf.at[k], sent_ref.at[me], load_sem.at[1]),
    )
    for own in kept:
        own.start()

    def finish(i, carry):
        s = lax.rem(me + count - i, count)
        gather_copy(s, s).wait_recv()
        return carry

    lax.fori_loop(1, count, finish, 0)

    def drain(i, carry):
        d = lax.rem(me + i, count)
        scatter_copy(d, me).wait_send()
        gather_copy(d, me).wait_send()
        return carry

    lax.fori_loop(1, count, drain, 0)
    for own in kept:
        own.wait()
    pair_b.wait_recv()
    pair_m.wait_send()
    pair_r.wait_send()
    pair_b.wait_send()


def exchange(
    count, column_weight, xblock, bank, filled, footprint, volume, extent, measured, ray
):
    slots = xblock.shape[1]
    operands = (xblock, bank, filled, footprint, volume, extent, measured, ray)
    angles = column_weight.shape[0]
    depth, _, total = volume.shape
    tiles = total // TILE
    banks = footprint.shape[0]
    m = angles * depth
    half = measured.shape[2] // 2
    pieces = (2, angles, depth, half)
    return pl.pallas_call(
        functools.partial(exchange_kernel, count),
        out_shape=(
            jax.ShapeDtypeStruct(measured.shape, jnp.float32),
            jax.ShapeDtypeStruct((count, m, half), jnp.bfloat16),
            jax.ShapeDtypeStruct((angles * slots, TILE), jnp.int32),
        ),
        in_specs=[SMEM] + [HBM] * len(operands),
        out_specs=(HBM, HBM, HBM),
        scratch_shapes=[pltpu.VMEM(x.shape, x.dtype) for x in operands]
        + [
            pltpu.VMEM((angles * slots, TILE), jnp.int32),
            pltpu.SMEM((angles * slots, TILE), jnp.int32),
            pltpu.SemaphoreType.DMA((len(operands) + 2,)),
            pltpu.VMEM((tiles * m, TILE), jnp.bfloat16),
            pltpu.VMEM(((banks + 1) * tiles * angles, ROWS, TILE), jnp.float32),
            pltpu.VMEM((count, m, half), jnp.bfloat16),
            pltpu.VMEM((count, m, half), jnp.bfloat16),
            pltpu.VMEM((2, m, half), jnp.float32),
            pltpu.VMEM(pieces, jnp.float32),
            pltpu.VMEM(pieces, jnp.float32),
            pltpu.VMEM(pieces, jnp.float32),
            pltpu.VMEM((2, m, half), jnp.bfloat16),
            pltpu.SemaphoreType.DMA((count,)),
            pltpu.SemaphoreType.DMA((count,)),
            pltpu.SemaphoreType.DMA((count,)),
            pltpu.SemaphoreType.DMA((count,)),
            pltpu.SemaphoreType.DMA((3,)),
            pltpu.SemaphoreType.DMA((3,)),
        ],
        compiler_params=pltpu.CompilerParams(
            collective_id=0, has_side_effects=True, vmem_limit_bytes=VMEM_LIMIT
        ),
        name="project_and_exchange",
    )(column_weight, *operands)


def shards(
    volume,
    column_weight,
    tile_xblock,
    tile_bank,
    tile_count,
    footprint,
    cone_extent,
    measured,
    ray_length,
):
    angles = column_weight.shape[0]
    depth, _, total = volume.shape
    tile_xblock = tile_xblock.transpose(0, 3, 1, 2)
    tile_bank = tile_bank.transpose(0, 3, 1, 2)
    half = measured.shape[2] // 2
    if lax.axis_size("gz") == 2 and half % TILE == 0:
        count = 2 * lax.axis_size("gy")
        back_rows, sent, packed = exchange(
            count,
            column_weight,
            tile_xblock,
            tile_bank,
            tile_count,
            footprint,
            volume,
            cone_extent,
            measured,
            ray_length,
        )
        new_volume, back_rows = back(
            packed, column_weight, sent, footprint, volume, back_rows
        )
    else:
        packed = packed_slots(tile_xblock, tile_bank, tile_count, footprint.shape[0])
        partial = forward(packed, column_weight, footprint, volume).reshape(angles, depth, total)
        owned = lax.psum_scatter(partial, "gy", scatter_dimension=2, tiled=True)
        predicted = cone_across(owned, cone_extent)
        back_rows = cone_across((measured - predicted) / ray_length, cone_extent)
        sent = lax.all_gather(back_rows.astype(jnp.bfloat16), "gy", axis=2, tiled=True)
        sent = sent.reshape(1, angles * depth, total)
        new_volume, back_rows = back(
            packed, column_weight, sent, footprint, volume, back_rows
        )
    return new_volume, back_rows


def solution(mesh):
    in_specs = (
        P(("parts", "gz"), "gy", None),
        P("parts", "gy"),
        P("parts", "gy", None, None),
        P("parts", "gy", None, None),
        P("parts", "gy", None),
        P(),
        P("parts", "gy"),
        P("parts", "gz", "gy"),
        P("parts", "gz", "gy"),
    )
    out_specs = (P(("parts", "gz"), "gy", None), P("parts", "gz", "gy"))
    return jax.shard_map(shards, mesh=mesh, in_specs=in_specs, out_specs=out_specs, check_vma=False)
```
